32 devices in a mesh: dp: 2 (over core), seq: 8 (over z, x), tp: 2 (over y).
Axes of the slice: x: 2, y: 2, z: 4, core: 2. Of those that a mesh axis runs over, the one named last changes fastest.
Arguments:
- projected: bfloat16 [4096, 3, 2048], P(('dp', 'seq'), None, 'tp'), may hold values from -24 to 24
- destinations: int32 [4096], P(('dp', 'seq')), may hold values from 0 to 7, as said below
- gather_ids: int32 [4096], P(('dp', 'seq')), may hold values from 0 to 63, as said below
- out_weight: bfloat16 [2048, 2048], P('tp'), may hold values from -0.125 to 0.125
- grad_output: bfloat16 [4096, 2048], P(('dp', 'seq'), 'tp'), may hold values from -6 to 6
Outputs:
- output: bfloat16 [4096, 2048], P(('dp', 'seq'), 'tp')
- grad_projected: bfloat16 [4096, 3, 2048], P(('dp', 'seq'), None, 'tp')
- grad_weight: float32 [2048, 2048], P('tp')
The draws below stay inside these ranges and needn't reach their ends.
Inputs may be any that keep to these rules, and one draw needn't show every extreme that they name: `destinations`: the 256 rows of one device form runs of 64 consecutive rows that name one sequence rank; the runs of one device name different ranks; in each dp index one rank is named by one run of every device. `gather_ids`: all rows of a run carry one gather number; a row packed into sequence rank r of dp index g carries a number from (g * 8 + r) * 4 to that plus 4 - 1.
All inputs are finite; a program needn't handle non-finite values.
Results may differ from the reference program's by a relative error of at most 0.022.
Values may be sent and summed in bfloat16 or wider, within the bound.
A program may use at most 128 MiB of HBM per device.

```python
import math
import jax
import jax.numpy as jnp
from jax import lax

D = 2048
H = 16
HD = 128
TOK_DEV = 256
GPR = 4
CAP = 64
TOKENS = 4096
N_SEQ = 8


def run_layout(key):
    group_count = TOKENS // (TOK_DEV * N_SEQ)
    run_total = TOK_DEV // CAP
    device_total = group_count * N_SEQ
    busy_rank = jax.random.randint(jax.random.fold_in(key, 101), (group_count,), 0, N_SEQ)
    busy_device = jnp.repeat(busy_rank, N_SEQ)
    other_keys = jax.random.split(jax.random.fold_in(key, 202), device_total)
    others = jax.vmap(lambda item: jax.random.permutation(item, N_SEQ - 1))(other_keys)[:, :run_total - 1]
    others = others + (others >= busy_device[:, None]).astype(jnp.int32)
    targets = jnp.concatenate([busy_device[:, None], others], axis=1).astype(jnp.int32)
    order_keys = jax.random.split(jax.random.fold_in(key, 303), device_total)
    orders = jax.vmap(lambda item: jax.random.permutation(item, run_total))(order_keys)
    targets = jnp.take_along_axis(targets, orders, axis=1)
    picked = jax.random.randint(jax.random.fold_in(key, 404), (device_total, run_total), 0, GPR)
    group_index = jnp.repeat(jnp.arange(group_count, dtype=jnp.int32), N_SEQ)[:, None]
    gathers = (group_index * N_SEQ + targets) * GPR + picked
    return (targets, gathers.astype(jnp.int32))


def draw_destinations(key, part):
    targets, gathers = run_layout(key)
    return jnp.repeat(targets.reshape(-1), CAP).astype(jnp.int32)


def draw_gather_ids(key, part):
    targets, gathers = run_layout(key)
    return jnp.repeat(gathers.reshape(-1), CAP).astype(jnp.int32)


def draw_projected(key, part):
    shape = (TOKENS, 3, H * HD)
    values = jnp.clip(jax.random.normal(key, shape, jnp.float32), -6.0, 6.0)
    return values.astype(jnp.bfloat16)


def shard_levels(stream_key, shape, pieces, smallest, high):
    level = 1.0
    for position, parts in pieces:
        steps = jax.random.uniform(jax.random.fold_in(jax.random.fold_in(stream_key, 6), position), (parts,), jnp.float32, smallest / len(pieces), high / len(pieces))
        level = level * jnp.repeat(jnp.exp(steps), shape[position] // parts).reshape((-1,) + (1,) * (len(shape) - 1 - position))
    return level


def centred(rng, extent, deviation, most, pieces=(), kind=jnp.bfloat16):
    values = jax.random.normal(rng, extent, jnp.float32) * deviation
    if len(pieces) > 0:
        values = shard_levels(rng, extent, pieces, -0.22, 0.18) * values
    return jnp.clip(values, min=-most, max=most).astype(kind)


def setup_inputs(seed: int = 0) -> dict:
    key_of = jax.random.split(jax.random.key(seed), 6)
    projected = draw_projected(jax.random.fold_in(key_of[5], 71), 0)
    destinations = draw_destinations(jax.random.fold_in(key_of[5], 71), 0)
    gather_ids = draw_gather_ids(jax.random.fold_in(key_of[5], 71), 0)
    out_weight = centred(key_of[3], (H * HD, D), (H * HD) ** -0.5, 0.125, ((0, 2),))
    grad_output = centred(key_of[4], (TOKENS, D), 1.0, 6.0, ((0, 16), (1, 2)))
    return {"projected": projected, "destinations": destinations, "gather_ids": gather_ids, "out_weight": out_weight, "grad_output": grad_output}


masked_score = -1e+30

def softmax_rows(query_all, key_all, slot_gather):
    scores = jnp.einsum('qhd,khd->hqk', query_all, key_all) * (1.0 / math.sqrt(HD))
    matching = slot_gather[:, None] == slot_gather[None, :]
    scores = jnp.where(matching[None], scores, masked_score)
    peak = lax.optimization_barrier(jnp.max(scores, axis=2, keepdims=True))
    raised = jnp.exp(scores - peak)
    return raised / lax.optimization_barrier(jnp.sum(raised, axis=2, keepdims=True))

def slot_rows(pair, run_target):
    group = pair // N_SEQ
    target = pair % N_SEQ
    matching = run_target[group] == target
    present = jnp.any(matching, axis=1)
    chosen = jnp.argmax(matching, axis=1).astype(jnp.int32)
    sources = jnp.arange(N_SEQ, dtype=jnp.int32)
    offsets = jnp.arange(CAP, dtype=jnp.int32)
    row_index = ((group * N_SEQ + sources) * TOK_DEV + chosen * CAP)[:, None] + offsets[None, :]
    present = jnp.broadcast_to(present[:, None], (N_SEQ, CAP)).reshape(-1)
    return (row_index.reshape(-1).astype(jnp.int32), present)

def reference(projected, destinations, gather_ids, out_weight, grad_output):
    group_count = TOKENS // (TOK_DEV * N_SEQ)
    run_count = TOK_DEV // CAP
    run_target = destinations.reshape(group_count, N_SEQ, run_count, CAP)[..., 0]
    width_all = H * HD
    scaling = 1.0 / math.sqrt(HD)
    pairs = jnp.arange(group_count * N_SEQ, dtype=jnp.int32)

    def gather_slots(pair):
        row_index, present = slot_rows(pair, run_target)
        inputs = jnp.where(present[:, None, None], projected[row_index], jnp.zeros((), projected.dtype))
        slot_gather = jnp.where(present, gather_ids[row_index], -1)
        dropped = jnp.where(present, row_index, TOKENS).astype(jnp.int32)
        return (inputs, slot_gather, dropped, present, row_index)

    def split_heads(inputs):
        full = inputs.astype(jnp.float32).reshape(N_SEQ * CAP, 3, H, HD)
        return (full[:, 0], full[:, 1], full[:, 2])

    def forward_step(attended_rows, pair):
        inputs, slot_gather, dropped, present, row_index = gather_slots(pair)
        query_all, key_all, value_all = split_heads(inputs)
        weights = softmax_rows(query_all, key_all, slot_gather)
        rounded = lax.optimization_barrier(weights.astype(jnp.bfloat16)).astype(jnp.float32)
        result = jnp.einsum('hqk,khd->qhd', rounded, value_all).reshape(-1, width_all).astype(jnp.bfloat16)
        attended_rows = attended_rows.at[dropped].set(result, mode='drop')
        return (attended_rows, None)
    start_rows = jnp.zeros((TOKENS, width_all), jnp.bfloat16)
    attended_rows, _ = lax.scan(forward_step, start_rows, pairs)
    output = jnp.dot(attended_rows, out_weight, preferred_element_type=jnp.float32).astype(jnp.bfloat16)
    grad_attended = jnp.dot(grad_output, out_weight.T, preferred_element_type=jnp.float32).astype(jnp.bfloat16)
    grad_weight = jnp.dot(attended_rows.T, grad_output, preferred_element_type=jnp.float32) / math.sqrt(TOKENS)

    def backward_step(grad_rows, pair):
        inputs, slot_gather, dropped, present, row_index = gather_slots(pair)
        query_all, key_all, value_all = split_heads(inputs)
        attended_slots = jnp.where(present[:, None], attended_rows[row_index], jnp.zeros((), attended_rows.dtype))
        attended_slots = attended_slots.astype(jnp.float32).reshape(-1, H, HD)
        grad_slots = jnp.where(present[:, None], grad_attended[row_index], jnp.zeros((), grad_attended.dtype))
        grad_slots = grad_slots.astype(jnp.float32).reshape(-1, H, HD)
        weights = softmax_rows(query_all, key_all, slot_gather)
        rounded = lax.optimization_barrier(weights.astype(jnp.bfloat16)).astype(jnp.float32)
        grad_weights = jnp.einsum('qhd,khd->hqk', grad_slots, value_all)
        delta = jnp.einsum('qhd,qhd->hq', grad_slots, attended_slots)[..., None]
        grad_scores = lax.optimization_barrier((weights * (grad_weights - delta)).astype(jnp.bfloat16)).astype(jnp.float32)
        grad_query = (jnp.einsum('hqk,khd->qhd', grad_scores, key_all) * scaling).astype(jnp.bfloat16)
        grad_key = (jnp.einsum('hqk,qhd->khd', grad_scores, query_all) * scaling).astype(jnp.bfloat16)
        grad_value = jnp.einsum('hqk,qhd->khd', rounded, grad_slots).astype(jnp.bfloat16)
        stacked = jnp.stack([grad_query, grad_key, grad_value], axis=1).reshape(-1, 3, width_all)
        grad_rows = grad_rows.at[dropped].set(stacked, mode='drop')
        return (grad_rows, None)
    start_grads = jnp.zeros((TOKENS, 3, width_all), jnp.bfloat16)
    grad_projected, _ = lax.scan(backward_step, start_grads, pairs)
    return (output, grad_projected, grad_weight)
```

```python
import functools
import math

import jax
import jax.numpy as jnp
from jax import lax
from jax.experimental import pallas as pl
from jax.experimental.pallas import tpu as pltpu
from jax.sharding import PartitionSpec as P

HD = 128
NEG = -1e30
BF = jnp.bfloat16
F32 = jnp.float32


def _dot(a, b, ca, cb):
    return lax.dot_general(a, b, (((ca,), (cb,)), ((), ())), preferred_element_type=F32)


def _attend_kernel(backward, ranks, run_count, run_rows, counts, order, gathers, *refs):
    if backward:
        x_ref, a_ref, g_ref, out_ref, key_acc, value_acc = refs
    else:
        x_ref, out_ref = refs
    scaling = 1.0 / math.sqrt(HD)

    def at(index):
        run = order[index]
        source = run // run_count
        start = pl.multiple_of((run % run_count) * run_rows, run_rows)
        return source, pl.ds(start, run_rows)

    def variant(rank, runs, query_runs):
        base = rank * ranks
        keys = runs * run_rows
        places = [at(base + j) for j in range(runs)]
        take = lambda part, span: jnp.concatenate([x_ref[s, part, d, :] for s, d in span], axis=0)
        key_all = take(1, places)
        value_all = take(2, places)
        lane_run = lax.broadcasted_iota(jnp.int32, (1, keys), 1) // run_rows
        key_gather = jnp.full((1, keys), gathers[base], jnp.int32)
        for j in range(1, runs):
            key_gather = jnp.where(lane_run == j, gathers[base + j], key_gather)
        for first in range(0, runs, query_runs):
            span = places[first : first + query_runs]
            query = take(0, span)
            bias = jnp.concatenate(
                [
                    jnp.broadcast_to(
                        jnp.where(key_gather == gathers[base + first + j], 0.0, NEG).astype(F32),
                        (run_rows, keys),
                    )
                    for j in range(query_runs)
                ],
                axis=0,
            )
            scores = _dot(query, key_all, 1, 1) * scaling + bias
            peak = jnp.max(scores, axis=1, keepdims=True)
            raised = jnp.exp(scores - peak)
            probs = raised * (1.0 / jnp.sum(raised, axis=1, keepdims=True))
            low = probs.astype(BF)
            if not backward:
                result = _dot(low, value_all, 1, 0).astype(BF)
                for j, (s, d) in enumerate(span):

                    @pl.when(first + j < counts[rank])
                    def _(s=s, d=d, j=j):
                        out_ref[s, d, :] = result[j * run_rows : (j + 1) * run_rows]

                continue
            grad = jnp.concatenate([g_ref[s, d, :] for s, d in span], axis=0)
            kept = jnp.concatenate([a_ref[s, d, :] for s, d in span], axis=0)
            grad_probs = _dot(grad, value_all, 1, 1)
            delta = jnp.sum(grad.astype(F32) * kept.astype(F32), axis=1, keepdims=True)
            grad_scores = (probs * (grad_probs - delta)).astype(BF)
            query_grad = (_dot(grad_scores, key_all, 1, 0) * scaling).astype(BF)
            for j, (s, d) in enumerate(span):

                @pl.when(first + j < counts[rank])
                def _(s=s, d=d, j=j):
                    out_ref[s, 0, d, :] = query_grad[j * run_rows : (j + 1) * run_rows]

            key_part = _dot(grad_scores, query, 0, 0)
            value_part = _dot(low, grad, 0, 0)
            if first + query_runs < runs:
                if first == 0:
                    key_acc[...] = key_part
                    value_acc[...] = value_part
                else:
                    key_acc[...] += key_part
                    value_acc[...] += value_part
                continue
            if first > 0:
                key_part = key_part + key_acc[...]
                value_part = value_part + value_acc[...]
            key_grad = (key_part * scaling).astype(BF)
            value_grad = value_part.astype(BF)
            for j, (s, d) in enumerate(places):

                @pl.when(j < counts[rank])
                def _(s=s, d=d, j=j):
                    rows = slice(j * run_rows, (j + 1) * run_rows)
                    out_ref[s, 1, d, :] = key_grad[rows]
                    out_ref[s, 2, d, :] = value_grad[rows]

    half = max(ranks // 2, 1)

    @pl.loop(0, ranks)
    def _(rank):
        @pl.when((counts[rank] > 0) & (counts[rank] <= half))
        def _():
            variant(rank, half, half)

        @pl.when(counts[rank] > half)
        def _():
            variant(rank, ranks, half)


def attend(backward, ranks, run_count, run_rows, tables, *arrays):
    rows = run_count * run_rows
    shape = (ranks, 3, rows, HD) if backward else (ranks, rows, HD)
    vmem = pl.BlockSpec(memory_space=pltpu.VMEM)
    scratch = [pltpu.VMEM((ranks * run_rows, HD), F32)] * 2 if backward else []
    return pl.pallas_call(
        functools.partial(_attend_kernel, backward, ranks, run_count, run_rows),
        out_shape=jax.ShapeDtypeStruct(shape, BF),
        grid_spec=pltpu.PrefetchScalarGridSpec(
            num_scalar_prefetch=3,
            grid=(),
            in_specs=[vmem] * len(arrays),
            out_specs=vmem,
            scratch_shapes=scratch,
        ),
        compiler_params=pltpu.CompilerParams(vmem_limit_bytes=40 * 1024 * 1024),
        cost_estimate=pl.CostEstimate(
            flops=(6 if backward else 2) * 10**8, bytes_accessed=3 * 10**6, transcendentals=10**6
        ),
        name="attend_back" if backward else "attend",
    )(*tables, *arrays)


def run_tables(run_target, run_gather, ranks):
    runs = run_target.shape[0]
    rank_ids = jnp.arange(ranks, dtype=jnp.int32)
    named = run_target[None, :] == rank_ids[:, None]
    counts = jnp.sum(named.astype(jnp.int32), axis=1)
    run_ids = jnp.arange(runs, dtype=jnp.int32)
    earlier = named[:, None, :] & (run_ids[None, None, :] < run_ids[None, :, None])
    place = jnp.sum(earlier.astype(jnp.int32), axis=2)
    hit = named[:, None, :] & (place[:, None, :] == rank_ids[None, :, None])
    order = jnp.sum(jnp.where(hit, run_ids, 0), axis=2)
    gathers = jnp.sum(jnp.where(hit, run_gather + 1, 0), axis=2) - 1
    return counts, order.reshape(-1), gathers.reshape(-1)


def swap_gather(values, axis_name):
    if lax.axis_size(axis_name) != 2:
        return lax.all_gather(values, axis_name, axis=1, tiled=True)
    other = lax.ppermute(values, axis_name, [(0, 1), (1, 0)])
    first = lax.axis_index(axis_name) == 0
    return jnp.where(
        first,
        jnp.concatenate([values, other], axis=1),
        jnp.concatenate([other, values], axis=1),
    )


def on_device(projected, destinations, gather_ids, out_weight, grad_output):
    ranks = lax.axis_size("seq")
    row_count = projected.shape[0]
    run_rows = 2 * row_count // ranks
    run_count = row_count // run_rows
    width = projected.shape[2]
    exchange = functools.partial(
        lax.all_to_all, axis_name="seq", split_axis=0, concat_axis=0, tiled=True
    )
    run_info = jnp.stack(
        [
            destinations.reshape(run_count, run_rows)[:, 0],
            gather_ids.reshape(run_count, run_rows)[:, 0],
        ]
    )
    info = exchange(jnp.broadcast_to(run_info[None], (ranks, 2, run_count)))
    info = info.transpose(1, 0, 2).reshape(2, ranks * run_count)
    x = projected.transpose(1, 0, 2).reshape(3, row_count, ranks, HD).transpose(2, 0, 1, 3)
    x = exchange(x)
    tables = run_tables(info[0], info[1], ranks)

    columns = swap_gather(grad_output, "tp")
    grad_rows = _dot(columns, out_weight, 1, 1).astype(BF)
    g = exchange(grad_rows.reshape(row_count, ranks, HD).transpose(1, 0, 2))

    attended = attend(False, ranks, run_count, run_rows, tables, x)
    attended_rows = exchange(attended).transpose(1, 0, 2).reshape(row_count, width)
    back = attend(True, ranks, run_count, run_rows, tables, x, attended, g)
    grads = exchange(back)
    grad_projected = grads.transpose(1, 2, 0, 3).reshape(3, row_count, width).transpose(1, 0, 2)

    output = project(attended_rows, out_weight)
    product = _dot(attended_rows, columns, 0, 0)
    row_total = row_count * lax.axis_size("dp") * ranks
    grad_weight = total_over_rows(product, 1.0 / math.sqrt(row_total))
    return output, grad_projected, grad_weight


def project(attended_rows, out_weight):
    partial_terms = _dot(attended_rows, out_weight, 1, 0)
    if lax.axis_size("tp") != 2:
        return lax.psum_scatter(partial_terms, "tp", scatter_dimension=1, tiled=True).astype(BF)
    half = out_weight.shape[1] // 2
    first = lax.axis_index("tp") == 0
    mine = jnp.where(first, partial_terms[:, :half], partial_terms[:, half:])
    sent = jnp.where(first, partial_terms[:, half:], partial_terms[:, :half]).astype(BF)
    other = lax.ppermute(sent, "tp", [(0, 1), (1, 0)])
    return (mine + other.astype(F32)).astype(BF)


def total_over_rows(product, factor):
    ranks = lax.axis_size("seq")
    half, columns = product.shape[0] // 2, product.shape[1]
    first = lax.axis_index("dp") == 0
    pairs = [(0, 1), (1, 0)]
    mine = jnp.where(first, product[:half], product[half:])
    sent = jnp.where(first, product[half:], product[:half]).astype(BF)
    mine = mine + lax.ppermute(sent, "dp", pairs).astype(F32)
    blocks = mine.astype(BF).reshape(ranks, half // ranks, columns)
    blocks = lax.all_to_all(blocks, "seq", split_axis=0, concat_axis=0, tiled=True)
    total = (jnp.sum(blocks.astype(F32), axis=0) * factor).astype(BF)
    total = lax.all_gather(total, "seq", axis=0, tiled=True)
    other = lax.ppermute(total, "dp", pairs)
    both = jnp.where(
        first, jnp.concatenate([total, other]), jnp.concatenate([other, total])
    )
    return both.astype(F32)


masked_score = -1e30


def packed_on_device(projected, destinations, gather_ids, out_weight, grad_output):
    rank_count = lax.axis_size("seq")
    row_count = projected.shape[0]
    run_rows = 2 * row_count // rank_count
    width_local = projected.shape[2]
    head_count = width_local // HD
    run_count = row_count // run_rows
    slot_count = rank_count * run_rows
    scaling = 1.0 / math.sqrt(HD)
    run_target = destinations.reshape(run_count, run_rows)[:, 0]
    run_gather = gather_ids.reshape(run_count, run_rows)[:, 0]
    picked_mask = run_target[None, :] == jnp.arange(rank_count, dtype=jnp.int32)[:, None]
    selector = picked_mask.astype(jnp.bfloat16)

    def pack_rows(values):
        features = values.shape[1]
        blocks = values.reshape(run_count, run_rows * features)
        packed = jnp.dot(selector, blocks, preferred_element_type=jnp.float32)
        return packed.astype(jnp.bfloat16).reshape(rank_count, run_rows, features)

    def unpack_rows(buffer):
        features = buffer.shape[2]
        flat = buffer.reshape(rank_count, run_rows * features)
        rows_back = lax.dot_general(
            selector, flat, (((0,), (0,)), ((), ())), preferred_element_type=jnp.float32
        )
        return rows_back.astype(jnp.bfloat16).reshape(row_count, features)

    slot_gather = jnp.where(
        jnp.any(picked_mask, axis=1),
        jnp.sum(jnp.where(picked_mask, run_gather[None, :], 0), axis=1),
        -1,
    )
    gather_send = jnp.broadcast_to(slot_gather[:, None], (rank_count, run_rows))
    packed_send = pack_rows(projected.reshape(row_count, 3 * width_local))
    received, received_ids = (
        lax.all_to_all(packed_send, "seq", split_axis=0, concat_axis=0, tiled=True),
        lax.all_to_all(gather_send, "seq", split_axis=0, concat_axis=0, tiled=True),
    )
    received = received.reshape(slot_count, 3, width_local)
    key_ids = received_ids.reshape(slot_count)
    matching = key_ids[:, None] == key_ids[None, :]

    def head_inputs(head_index):
        lower = head_index * HD
        return (
            received[:, 0, lower : lower + HD],
            received[:, 1, lower : lower + HD],
            received[:, 2, lower : lower + HD],
        )

    def probabilities(query_head, key_head):
        scores = (
            lax.dot_general(
                query_head, key_head, (((1,), (1,)), ((), ())), preferred_element_type=jnp.float32
            )
            * scaling
        )
        scores = jnp.where(matching, scores, masked_score)
        peak = jnp.max(scores, axis=1, keepdims=True)
        raised = jnp.exp(scores - peak)
        return raised / jnp.sum(raised, axis=1, keepdims=True)

    results = []
    for head_index in range(head_count):
        query_head, key_head, value_head = head_inputs(head_index)
        weights = probabilities(query_head, key_head).astype(jnp.bfloat16)
        results.append(
            jnp.dot(weights, value_head, preferred_element_type=jnp.float32).astype(jnp.bfloat16)
        )
    attended = jnp.concatenate(results, axis=1)
    returned = lax.all_to_all(
        attended.reshape(rank_count, run_rows, width_local),
        "seq",
        split_axis=0,
        concat_axis=0,
        tiled=True,
    )
    attended_rows = unpack_rows(returned)
    partial_terms = jnp.dot(attended_rows, out_weight, preferred_element_type=jnp.float32)
    output = lax.psum_scatter(partial_terms, "tp", scatter_dimension=1, tiled=True).astype(
        jnp.bfloat16
    )
    shard_cols = lax.all_gather(grad_output, "tp", axis=1, tiled=True)
    grad_rows = lax.dot_general(
        shard_cols, out_weight, (((1,), (1,)), ((), ())), preferred_element_type=jnp.float32
    )
    product = lax.dot_general(
        attended_rows, shard_cols, (((0,), (0,)), ((), ())), preferred_element_type=jnp.float32
    )
    grad_block = product
    grad_rows, grad_block = (grad_rows, grad_block)
    row_total = row_count * lax.axis_size("dp") * rank_count
    grad_weight = lax.psum(grad_block, ("dp", "seq")) * (1.0 / math.sqrt(row_total))
    grad_attended = grad_rows.astype(jnp.bfloat16)
    grad_slots = lax.all_to_all(
        pack_rows(grad_attended), "seq", split_axis=0, concat_axis=0, tiled=True
    )
    grad_slots = grad_slots.reshape(slot_count, width_local)
    query_grads = []
    key_grads = []
    value_grads = []
    for head_index in range(head_count):
        query_head, key_head, value_head = head_inputs(head_index)
        lower = head_index * HD
        grad_head = grad_slots[:, lower : lower + HD]
        result_head = attended[:, lower : lower + HD]
        weights = probabilities(query_head, key_head)
        weights_low = weights.astype(jnp.bfloat16)
        grad_weights = lax.dot_general(
            grad_head, value_head, (((1,), (1,)), ((), ())), preferred_element_type=jnp.float32
        )
        delta = jnp.sum(
            grad_head.astype(jnp.float32) * result_head.astype(jnp.float32), axis=1, keepdims=True
        )
        grad_scores = (weights * (grad_weights - delta)).astype(jnp.bfloat16)
        query_grads.append(
            (jnp.dot(grad_scores, key_head, preferred_element_type=jnp.float32) * scaling).astype(
                jnp.bfloat16
            )
        )
        key_grads.append(
            (
                lax.dot_general(
                    grad_scores,
                    query_head,
                    (((0,), (0,)), ((), ())),
                    preferred_element_type=jnp.float32,
                )
                * scaling
            ).astype(jnp.bfloat16)
        )
        value_grads.append(
            lax.dot_general(
                weights_low, grad_head, (((0,), (0,)), ((), ())), preferred_element_type=jnp.float32
            ).astype(jnp.bfloat16)
        )
    stacked = jnp.stack(
        [
            jnp.concatenate(query_grads, axis=1),
            jnp.concatenate(key_grads, axis=1),
            jnp.concatenate(value_grads, axis=1),
        ],
        axis=1,
    )
    grads_back = lax.all_to_all(
        stacked.reshape(rank_count, run_rows, 3 * width_local),
        "seq",
        split_axis=0,
        concat_axis=0,
        tiled=True,
    )
    grad_projected = unpack_rows(grads_back).reshape(row_count, 3, width_local)
    return (output, grad_projected, grad_weight)


def solution(mesh):
    placed = (
        P(("dp", "seq"), None, "tp"),
        P(("dp", "seq")),
        P(("dp", "seq")),
        P("tp", None),
        P(("dp", "seq"), "tp"),
    )
    whole_heads = 2048 // HD // mesh.shape["tp"] == mesh.shape["seq"]
    return jax.shard_map(
        on_device if whole_heads else packed_on_device,
        mesh=mesh,
        in_specs=placed,
        out_specs=(P(("dp", "seq"), "tp"), P(("dp", "seq"), None, "tp"), P("tp", None)),
        check_vma=False,
    )
```

```python
import functools
import math

import jax
import jax.numpy as jnp
from jax import lax
from jax.experimental import pallas as pl
from jax.experimental.pallas import tpu as pltpu
from jax.sharding import PartitionSpec as P

HD = 128
NEG = -1e30
BF = jnp.bfloat16
F32 = jnp.float32


def _dot(a, b, ca, cb):
    return lax.dot_general(a, b, (((ca,), (cb,)), ((), ())), preferred_element_type=F32)


def _attend_kernel(backward, ranks, run_count, run_rows, counts, order, gathers, *refs):
    if backward:
        x_ref, a_ref, g_ref, out_ref, key_acc, value_acc = refs
    else:
        x_ref, out_ref = refs
    scaling = 1.0 / math.sqrt(HD)
    rows = run_count * run_rows

    def at(index):
        run = order[index]
        source = run // run_count
        start = pl.multiple_of((run % run_count) * run_rows, run_rows)
        return source, pl.ds(start, run_rows)

    def variant(rank, runs, query_runs):
        base = rank * ranks
        keys = runs * run_rows
        places = [at(base + j) for j in range(runs)]
        take = lambda part, span: jnp.concatenate(
            [x_ref[s, pl.ds(part * rows + d.start, run_rows), :] for s, d in span], axis=0
        )
        key_all = take(1, places)
        value_all = take(2, places)
        lane_run = lax.broadcasted_iota(jnp.int32, (1, keys), 1) // run_rows
        key_gather = jnp.full((1, keys), gathers[base], jnp.int32)
        for j in range(1, runs):
            key_gather = jnp.where(lane_run == j, gathers[base + j], key_gather)
        for first in range(0, runs, query_runs):
            span = places[first : first + query_runs]
            query = take(0, span)
            bias = jnp.concatenate(
                [
                    jnp.broadcast_to(
                        jnp.where(key_gather == gathers[base + first + j], 0.0, NEG).astype(F32),
                        (run_rows, keys),
                    )
                    for j in range(query_runs)
                ],
                axis=0,
            )
            scores = _dot(query, key_all, 1, 1) * scaling + bias
            peak = jnp.max(scores, axis=1, keepdims=True)
            raised = jnp.exp(scores - peak)
            probs = raised * (1.0 / jnp.sum(raised, axis=1, keepdims=True))
            low = probs.astype(BF)
            if not backward:
                result = _dot(low, value_all, 1, 0).astype(BF)
                for j, (s, d) in enumerate(span):

                    @pl.when(first + j < counts[rank])
                    def _(s=s, d=d, j=j):
                        out_ref[s, d, :] = result[j * run_rows : (j + 1) * run_rows]

                continue
            grad = jnp.concatenate([g_ref[s, d, :] for s, d in span], axis=0)
            kept = jnp.concatenate([a_ref[s, d, :] for s, d in span], axis=0)
            grad_probs = _dot(grad, value_all, 1, 1)
            delta = jnp.sum(grad.astype(F32) * kept.astype(F32), axis=1, keepdims=True)
            grad_scores = (probs * (grad_probs - delta)).astype(BF)
            query_grad = (_dot(grad_scores, key_all, 1, 0) * scaling).astype(BF)
            for j, (s, d) in enumerate(span):

                @pl.when(first + j < counts[rank])
                def _(s=s, d=d, j=j):
                    out_ref[s, 0, d, :] = query_grad[j * run_rows : (j + 1) * run_rows]

            key_part = _dot(grad_scores, query, 0, 0)
            value_part = _dot(low, grad, 0, 0)
            if first + query_runs < runs:
                if first == 0:
                    key_acc[...] = key_part
                    value_acc[...] = value_part
                else:
                    key_acc[...] += key_part
                    value_acc[...] += value_part
                continue
            if first > 0:
                key_part = key_part + key_acc[...]
                value_part = value_part + value_acc[...]
            key_grad = (key_part * scaling).astype(BF)
            value_grad = value_part.astype(BF)
            for j, (s, d) in enumerate(places):

                @pl.when(j < counts[rank])
                def _(s=s, d=d, j=j):
                    rows = slice(j * run_rows, (j + 1) * run_rows)
                    out_ref[s, 1, d, :] = key_grad[rows]
                    out_ref[s, 2, d, :] = value_grad[rows]

    half = max(ranks // 2, 1)

    @pl.loop(0, ranks)
    def _(rank):
        @pl.when((counts[rank] > 0) & (counts[rank] <= half))
        def _():
            variant(rank, half, half)

        @pl.when(counts[rank] > half)
        def _():
            variant(rank, ranks, half)


def attend(backward, ranks, run_count, run_rows, tables, *arrays):
    rows = run_count * run_rows
    shape = (ranks, 3, rows, HD) if backward else (ranks, rows, HD)
    vmem = pl.BlockSpec(memory_space=pltpu.VMEM)
    scratch = [pltpu.VMEM((ranks * run_rows, HD), F32)] * 2 if backward else []
    return pl.pallas_call(
        functools.partial(_attend_kernel, backward, ranks, run_count, run_rows),
        out_shape=jax.ShapeDtypeStruct(shape, BF),
        grid_spec=pltpu.PrefetchScalarGridSpec(
            num_scalar_prefetch=3,
            grid=(),
            in_specs=[vmem] * len(arrays),
            out_specs=vmem,
            scratch_shapes=scratch,
        ),
        compiler_params=pltpu.CompilerParams(vmem_limit_bytes=40 * 1024 * 1024),
        cost_estimate=pl.CostEstimate(
            flops=(6 if backward else 2) * 10**8, bytes_accessed=3 * 10**6, transcendentals=10**6
        ),
        name="attend_back" if backward else "attend",
    )(*tables, *arrays)


def run_tables(run_target, run_gather, ranks):
    runs = run_target.shape[0]
    rank_ids = jnp.arange(ranks, dtype=jnp.int32)
    named = run_target[None, :] == rank_ids[:, None]
    counts = jnp.sum(named.astype(jnp.int32), axis=1)
    run_ids = jnp.arange(runs, dtype=jnp.int32)
    earlier = named[:, None, :] & (run_ids[None, None, :] < run_ids[None, :, None])
    place = jnp.sum(earlier.astype(jnp.int32), axis=2)
    hit = named[:, None, :] & (place[:, None, :] == rank_ids[None, :, None])
    order = jnp.sum(jnp.where(hit, run_ids, 0), axis=2)
    gathers = jnp.sum(jnp.where(hit, run_gather + 1, 0), axis=2) - 1
    return counts, order.reshape(-1), gathers.reshape(-1)


def swap_gather(values, axis_name):
    if lax.axis_size(axis_name) != 2:
        return lax.all_gather(values, axis_name, axis=1, tiled=True)
    other = lax.ppermute(values, axis_name, [(0, 1), (1, 0)])
    first = lax.axis_index(axis_name) == 0
    return jnp.where(
        first,
        jnp.concatenate([values, other], axis=1),
        jnp.concatenate([other, values], axis=1),
    )


def on_device(projected, destinations, gather_ids, out_weight, grad_output):
    ranks = lax.axis_size("seq")
    row_count = projected.shape[0]
    run_rows = 2 * row_count // ranks
    run_count = row_count // run_rows
    width = projected.shape[2]
    exchange = functools.partial(
        lax.all_to_all, axis_name="seq", split_axis=0, concat_axis=0, tiled=True
    )
    run_info = jnp.concatenate(
        [
            destinations.reshape(run_count, run_rows)[:, 0],
            gather_ids.reshape(run_count, run_rows)[:, 0],
        ]
    )
    tail = jnp.broadcast_to(jnp.pad(run_info, (0, HD - 2 * run_count))[None, :], (16, HD))
    x = exchange(split_heads(projected.transpose(1, 0, 2), tail.astype(BF), ranks))
    info = x[:, 3 * row_count, : 2 * run_count].astype(jnp.int32)
    run_target = info[:, :run_count].reshape(-1)
    run_gather = info[:, run_count:].reshape(-1)
    tables = run_tables(run_target, run_gather, ranks)

    columns = swap_gather(grad_output, "tp")
    grad_rows = _dot(columns, out_weight, 1, 1).astype(BF)
    blocks = head_blocks(grad_rows, ranks)
    x, blocks, columns = lax.optimization_barrier((x, blocks, columns))
    g = exchange(blocks)

    attended = attend(False, ranks, run_count, run_rows, tables, x)
    attended_rows = exchange(attended)
    back = attend(True, ranks, run_count, run_rows, tables, x, attended, g)
    attended_rows, back = lax.optimization_barrier((attended_rows, back))
    grads = exchange(back)
    attended_rows = jnp.concatenate([attended_rows[h] for h in range(ranks)], axis=1)

    partial_terms = _dot(attended_rows, out_weight, 1, 0)
    product = _dot(attended_rows, columns, 0, 0)
    row_total = row_count * lax.axis_size("dp") * ranks
    half = out_weight.shape[1] // 2
    first = lax.axis_index("tp") == 0
    mine = jnp.where(first, partial_terms[:, :half], partial_terms[:, half:])
    sent = jnp.where(first, partial_terms[:, half:], partial_terms[:, :half]).astype(BF)
    other, total = reduce_sums(sent, product, ranks, 1.0 / math.sqrt(row_total))
    output = (mine + other.astype(F32)).astype(BF)
    grad_projected = join_heads(grads, row_count).transpose(1, 0, 2)
    return output, grad_projected, total.astype(F32)


def head_blocks(values, ranks):
    return jnp.stack([values[:, h * HD : (h + 1) * HD] for h in range(ranks)])


def _split_kernel(ranks, x_ref, tail_ref, out_ref):
    rows = x_ref.shape[1]
    for head in range(ranks):
        for part in range(3):
            block = x_ref[part, :, head * HD : (head + 1) * HD]
            out_ref[head, part * rows : (part + 1) * rows, :] = block
        out_ref[head, 3 * rows :, :] = tail_ref[...]


def split_heads(x, tail, ranks):
    vmem = pl.BlockSpec(memory_space=pltpu.VMEM)
    return pl.pallas_call(
        functools.partial(_split_kernel, ranks),
        out_shape=jax.ShapeDtypeStruct((ranks, 3 * x.shape[1] + tail.shape[0], HD), BF),
        in_specs=[vmem] * 2,
        out_specs=vmem,
        compiler_params=pltpu.CompilerParams(vmem_limit_bytes=24 * 1024 * 1024),
        cost_estimate=pl.CostEstimate(flops=0, bytes_accessed=4 * x.size, transcendentals=0),
        name="split_heads",
    )(x, tail)


def _join_kernel(x_ref, out_ref):
    for head in range(x_ref.shape[0]):
        for part in range(3):
            out_ref[part, :, head * HD : (head + 1) * HD] = x_ref[head, part]


def join_heads(x, rows):
    vmem = pl.BlockSpec(memory_space=pltpu.VMEM)
    return pl.pallas_call(
        _join_kernel,
        out_shape=jax.ShapeDtypeStruct((3, rows, x.shape[0] * HD), BF),
        in_specs=[vmem],
        out_specs=vmem,
        compiler_params=pltpu.CompilerParams(vmem_limit_bytes=24 * 1024 * 1024),
        cost_estimate=pl.CostEstimate(flops=0, bytes_accessed=4 * x.size, transcendentals=0),
        name="join_heads",
    )(x)


def _reduce_kernel(
    ranks, factor, sent_ref, product_ref, other_ref, out_ref, pair_out, pair_in, first_out, ring_in,
    tp_send, tp_recv, pair_send, pair_recv, sum_send, sum_recv, all_send, all_recv, last_send, last_recv
):
    core, seq, tp = lax.axis_index("dp"), lax.axis_index("seq"), lax.axis_index("tp")
    half, columns = product_ref.shape[0] // 2, product_ref.shape[1]
    chunk, wide = half // ranks, columns // 2
    mesh = pl.DeviceIdType.MESH

    def flip(index):
        z, x = index // 2, index % 2
        return z + x * (ranks - 1 - 2 * z)

    def unflip(place):
        x = place // (ranks // 2)
        return 2 * (place + x * (ranks - 1 - 2 * place)) + x

    me = flip(seq)
    ring = ({"seq": unflip((me + 1) % ranks)}, {"seq": unflip((me + ranks - 1) % ranks)})
    partner, across = {"dp": 1 - core}, {"tp": 1 - tp}

    barrier = pltpu.get_barrier_semaphore()
    for device in (*ring, partner, across):
        pl.semaphore_signal(barrier, inc=1, device_id=device, device_id_type=mesh)
    pl.semaphore_wait(barrier, 4)

    def send(source, target, send_sem, recv_sem, device):
        copy = pltpu.make_async_remote_copy(
            src_ref=source, dst_ref=target, send_sem=send_sem, recv_sem=recv_sem,
            device_id=device, device_id_type=mesh,
        )
        copy.start()
        return copy

    def place(offset):
        return (me + offset + ranks) % ranks

    def chunk_rows(start, index):
        return pl.ds(pl.multiple_of(start + index * chunk, chunk), chunk)

    offsets = sorted(range(1, ranks), key=lambda o: (min(o, ranks - o), o)) + [0]
    pair = {}
    for slot, offset in enumerate(offsets):
        rows = chunk_rows((1 - core) * half, place(offset))
        pair_out[slot] = product_ref[rows, :].astype(BF)
        pair[offset] = (
            slot,
            send(pair_out.at[slot], pair_in.at[slot], pair_send.at[slot], pair_recv.at[slot], partner),
        )
    crossing = send(sent_ref, other_ref, tp_send, tp_recv, across)
    here = set()

    def own(offset, cols):
        offset = offset % ranks
        slot, copy = pair[offset]
        if offset not in here:
            here.add(offset)
            copy.wait_recv()
        rows = chunk_rows(core * half, place(offset))
        return product_ref[rows, cols] + pair_in[slot, :, cols].astype(F32)

    cols = (slice(0, wide), slice(wide, columns))
    copies = []
    moving = [None, None]
    for way in range(2):
        sign = -1 if way == 0 else 1
        first_out[way] = own(sign, cols[way]).astype(BF)
        moving[way] = send(
            first_out.at[way], ring_in.at[way, 0], sum_send.at[way, 0], sum_recv.at[way, 0], ring[way]
        )
        copies.append(moving[way])
    for step in range(1, ranks):
        for way in range(2):
            sign = -1 if way == 0 else 1
            mine = own(sign * (step + 1), cols[way])
            moving[way].wait_recv()
            value = mine + ring_in[way, step - 1].astype(F32)
            if step < ranks - 1:
                ring_in[way, step - 1] = value.astype(BF)
                moving[way] = send(
                    ring_in.at[way, step - 1], ring_in.at[way, step],
                    sum_send.at[way, step], sum_recv.at[way, step], ring[way],
                )
                copies.append(moving[way])
            else:
                out_ref[chunk_rows(core * half, me), cols[way]] = (value * factor).astype(BF)

    arrived = [None, None]
    finals = []
    for step in range(ranks):
        for way in range(2):
            sign = -1 if way == 0 else 1
            if step > 0:
                arrived[way].wait_recv()
            view = out_ref.at[chunk_rows(core * half, place(sign * step)), cols[way]]
            if step < ranks - 1:
                arrived[way] = send(view, view, all_send.at[way, step], all_recv.at[way, step], ring[way])
                copies.append(arrived[way])
            final = send(view, view, last_send.at[way, step], last_recv.at[way, step], partner)
            finals.append(final)
    for copy in copies:
        copy.wait_send()
    for _, copy in pair.values():
        copy.wait_send()
    for copy in finals:
        copy.wait()
    crossing.wait()


def reduce_sums(sent, product, ranks, factor):
    half, columns = product.shape[0] // 2, product.shape[1]
    chunk = half // ranks
    dma = pltpu.SemaphoreType.DMA
    vmem = pl.BlockSpec(memory_space=pltpu.VMEM)
    return pl.pallas_call(
        functools.partial(_reduce_kernel, ranks, factor),
        out_shape=(
            jax.ShapeDtypeStruct(sent.shape, BF),
            jax.ShapeDtypeStruct(product.shape, BF),
        ),
        in_specs=[vmem] * 2,
        out_specs=(vmem, vmem),
        scratch_shapes=[
            pltpu.VMEM((ranks, chunk, columns), BF),
            pltpu.VMEM((ranks, chunk, columns), BF),
            pltpu.VMEM((2, chunk, columns // 2), BF),
            pltpu.VMEM((2, ranks - 1, chunk, columns // 2), BF),
            dma, dma,
            *[dma((ranks,))] * 2,
            *[dma((2, ranks))] * 6,
        ],
        compiler_params=pltpu.CompilerParams(
            collective_id=0, has_side_effects=True, vmem_limit_bytes=40 * 1024 * 1024
        ),
        cost_estimate=pl.CostEstimate(flops=6 * 10**10, bytes_accessed=2 * 10**7, transcendentals=0),
        name="reduce_sums",
    )(sent, product)


masked_score = -1e30


def packed_on_device(projected, destinations, gather_ids, out_weight, grad_output):
    rank_count = lax.axis_size("seq")
    row_count = projected.shape[0]
    run_rows = 2 * row_count // rank_count
    width_local = projected.shape[2]
    head_count = width_local // HD
    run_count = row_count // run_rows
    slot_count = rank_count * run_rows
    scaling = 1.0 / math.sqrt(HD)
    run_target = destinations.reshape(run_count, run_rows)[:, 0]
    run_gather = gather_ids.reshape(run_count, run_rows)[:, 0]
    picked_mask = run_target[None, :] == jnp.arange(rank_count, dtype=jnp.int32)[:, None]
    selector = picked_mask.astype(jnp.bfloat16)

    def pack_rows(values):
        features = values.shape[1]
        blocks = values.reshape(run_count, run_rows * features)
        packed = jnp.dot(selector, blocks, preferred_element_type=jnp.float32)
        return packed.astype(jnp.bfloat16).reshape(rank_count, run_rows, features)

    def unpack_rows(buffer):
        features = buffer.shape[2]
        flat = buffer.reshape(rank_count, run_rows * features)
        rows_back = lax.dot_general(
            selector, flat, (((0,), (0,)), ((), ())), preferred_element_type=jnp.float32
        )
        return rows_back.astype(jnp.bfloat16).reshape(row_count, features)

    slot_gather = jnp.where(
        jnp.any(picked_mask, axis=1),
        jnp.sum(jnp.where(picked_mask, run_gather[None, :], 0), axis=1),
        -1,
    )
    gather_send = jnp.broadcast_to(slot_gather[:, None], (rank_count, run_rows))
    packed_send = pack_rows(projected.reshape(row_count, 3 * width_local))
    received, received_ids = (
        lax.all_to_all(packed_send, "seq", split_axis=0, concat_axis=0, tiled=True),
        lax.all_to_all(gather_send, "seq", split_axis=0, concat_axis=0, tiled=True),
    )
    received = received.reshape(slot_count, 3, width_local)
    key_ids = received_ids.reshape(slot_count)
    matching = key_ids[:, None] == key_ids[None, :]

    def head_inputs(head_index):
        lower = head_index * HD
        return (
            received[:, 0, lower : lower + HD],
            received[:, 1, lower : lower + HD],
            received[:, 2, lower : lower + HD],
        )

    def probabilities(query_head, key_head):
        scores = (
            lax.dot_general(
                query_head, key_head, (((1,), (1,)), ((), ())), preferred_element_type=jnp.float32
            )
            * scaling
        )
        scores = jnp.where(matching, scores, masked_score)
        peak = jnp.max(scores, axis=1, keepdims=True)
        raised = jnp.exp(scores - peak)
        return raised / jnp.sum(raised, axis=1, keepdims=True)

    results = []
    for head_index in range(head_count):
        query_head, key_head, value_head = head_inputs(head_index)
        weights = probabilities(query_head, key_head).astype(jnp.bfloat16)
        results.append(
            jnp.dot(weights, value_head, preferred_element_type=jnp.float32).astype(jnp.bfloat16)
        )
    attended = jnp.concatenate(results, axis=1)
    returned = lax.all_to_all(
        attended.reshape(rank_count, run_rows, width_local),
        "seq",
        split_axis=0,
        concat_axis=0,
        tiled=True,
    )
    attended_rows = unpack_rows(returned)
    partial_terms = jnp.dot(attended_rows, out_weight, preferred_element_type=jnp.float32)
    output = lax.psum_scatter(partial_terms, "tp", scatter_dimension=1, tiled=True).astype(
        jnp.bfloat16
    )
    shard_cols = lax.all_gather(grad_output, "tp", axis=1, tiled=True)
    grad_rows = lax.dot_general(
        shard_cols, out_weight, (((1,), (1,)), ((), ())), preferred_element_type=jnp.float32
    )
    product = lax.dot_general(
        attended_rows, shard_cols, (((0,), (0,)), ((), ())), preferred_element_type=jnp.float32
    )
    grad_block = product
    grad_rows, grad_block = (grad_rows, grad_block)
    row_total = row_count * lax.axis_size("dp") * rank_count
    grad_weight = lax.psum(grad_block, ("dp", "seq")) * (1.0 / math.sqrt(row_total))
    grad_attended = grad_rows.astype(jnp.bfloat16)
    grad_slots = lax.all_to_all(
        pack_rows(grad_attended), "seq", split_axis=0, concat_axis=0, tiled=True
    )
    grad_slots = grad_slots.reshape(slot_count, width_local)
    query_grads = []
    key_grads = []
    value_grads = []
    for head_index in range(head_count):
        query_head, key_head, value_head = head_inputs(head_index)
        lower = head_index * HD
        grad_head = grad_slots[:, lower : lower + HD]
        result_head = attended[:, lower : lower + HD]
        weights = probabilities(query_head, key_head)
        weights_low = weights.astype(jnp.bfloat16)
        grad_weights = lax.dot_general(
            grad_head, value_head, (((1,), (1,)), ((), ())), preferred_element_type=jnp.float32
        )
        delta = jnp.sum(
            grad_head.astype(jnp.float32) * result_head.astype(jnp.float32), axis=1, keepdims=True
        )
        grad_scores = (weights * (grad_weights - delta)).astype(jnp.bfloat16)
        query_grads.append(
            (jnp.dot(grad_scores, key_head, preferred_element_type=jnp.float32) * scaling).astype(
                jnp.bfloat16
            )
        )
        key_grads.append(
            (
                lax.dot_general(
                    grad_scores,
                    query_head,
                    (((0,), (0,)), ((), ())),
                    preferred_element_type=jnp.float32,
                )
                * scaling
            ).astype(jnp.bfloat16)
        )
        value_grads.append(
            lax.dot_general(
                weights_low, grad_head, (((0,), (0,)), ((), ())), preferred_element_type=jnp.float32
            ).astype(jnp.bfloat16)
        )
    stacked = jnp.stack(
        [
            jnp.concatenate(query_grads, axis=1),
            jnp.concatenate(key_grads, axis=1),
            jnp.concatenate(value_grads, axis=1),
        ],
        axis=1,
    )
    grads_back = lax.all_to_all(
        stacked.reshape(rank_count, run_rows, 3 * width_local),
        "seq",
        split_axis=0,
        concat_axis=0,
        tiled=True,
    )
    grad_projected = unpack_rows(grads_back).reshape(row_count, 3, width_local)
    return (output, grad_projected, grad_weight)


def solution(mesh):
    placed = (
        P(("dp", "seq"), None, "tp"),
        P(("dp", "seq")),
        P(("dp", "seq")),
        P("tp", None),
        P(("dp", "seq"), "tp"),
    )
    sizes = mesh.shape
    whole_heads = 2048 // HD // sizes["tp"] == sizes["seq"] and sizes["tp"] == 2 == sizes["dp"]
    return jax.shard_map(
        on_device if whole_heads else packed_on_device,
        mesh=mesh,
        in_specs=placed,
        out_specs=(P(("dp", "seq"), "tp"), P(("dp", "seq"), None, "tp"), P("tp", None)),
        check_vma=False,
    )
```

```python
import functools
import math

import jax
import jax.numpy as jnp
from jax import lax
from jax.experimental import pallas as pl
from jax.experimental.pallas import tpu as pltpu
from jax.sharding import PartitionSpec as P

HD = 128
NEG = -1e30
BF = jnp.bfloat16
F32 = jnp.float32


def _dot(a, b, ca, cb):
    return lax.dot_general(a, b, (((ca,), (cb,)), ((), ())), preferred_element_type=F32)


def _attend_kernel(backward, ranks, run_count, run_rows, counts, order, gathers, *refs):
    if backward:
        x_ref, a_ref, g_ref, out_ref, key_acc, value_acc = refs
    else:
        x_ref, out_ref = refs
    scaling = 1.0 / math.sqrt(HD)
    rows = run_count * run_rows

    def at(index):
        run = order[index]
        source = run // run_count
        start = pl.multiple_of((run % run_count) * run_rows, run_rows)
        return source, pl.ds(start, run_rows)

    def variant(rank, runs, query_runs):
        base = rank * ranks
        keys = runs * run_rows
        places = [at(base + j) for j in range(runs)]
        take = lambda part, span: jnp.concatenate(
            [x_ref[s, pl.ds(part * rows + d.start, run_rows), :] for s, d in span], axis=0
        )
        key_all = take(1, places)
        value_all = take(2, places)
        lane_run = lax.broadcasted_iota(jnp.int32, (1, keys), 1) // run_rows
        key_gather = jnp.full((1, keys), gathers[base], jnp.int32)
        for j in range(1, runs):
            key_gather = jnp.where(lane_run == j, gathers[base + j], key_gather)
        for first in range(0, runs, query_runs):
            span = places[first : first + query_runs]
            query = take(0, span)
            bias = jnp.concatenate(
                [
                    jnp.broadcast_to(
                        jnp.where(key_gather == gathers[base + first + j], 0.0, NEG).astype(F32),
                        (run_rows, keys),
                    )
                    for j in range(query_runs)
                ],
                axis=0,
            )
            scores = _dot(query, key_all, 1, 1) * scaling + bias
            peak = jnp.max(scores, axis=1, keepdims=True)
            raised = jnp.exp(scores - peak)
            probs = raised * (1.0 / jnp.sum(raised, axis=1, keepdims=True))
            low = probs.astype(BF)
            if not backward:
                result = _dot(low, value_all, 1, 0).astype(BF)
                for j, (s, d) in enumerate(span):

                    @pl.when(first + j < counts[rank])
                    def _(s=s, d=d, j=j):
                        out_ref[s, d, :] = result[j * run_rows : (j + 1) * run_rows]

                continue
            grad = jnp.concatenate([g_ref[s, d, :] for s, d in span], axis=0)
            kept = jnp.concatenate([a_ref[s, d, :] for s, d in span], axis=0)
            grad_probs = _dot(grad, value_all, 1, 1)
            delta = jnp.sum(grad.astype(F32) * kept.astype(F32), axis=1, keepdims=True)
            grad_scores = (probs * (grad_probs - delta)).astype(BF)
            query_grad = (_dot(grad_scores, key_all, 1, 0) * scaling).astype(BF)
            for j, (s, d) in enumerate(span):

                @pl.when(first + j < counts[rank])
                def _(s=s, d=d, j=j):
                    out_ref[s, 0, d, :] = query_grad[j * run_rows : (j + 1) * run_rows]

            key_part = _dot(grad_scores, query, 0, 0)
            value_part = _dot(low, grad, 0, 0)
            if first + query_runs < runs:
                if first == 0:
                    key_acc[...] = key_part
                    value_acc[...] = value_part
                else:
                    key_acc[...] += key_part
                    value_acc[...] += value_part
                continue
            if first > 0:
                key_part = key_part + key_acc[...]
                value_part = value_part + value_acc[...]
            key_grad = (key_part * scaling).astype(BF)
            value_grad = value_part.astype(BF)
            for j, (s, d) in enumerate(places):

                @pl.when(j < counts[rank])
                def _(s=s, d=d, j=j):
                    rows = slice(j * run_rows, (j + 1) * run_rows)
                    out_ref[s, 1, d, :] = key_grad[rows]
                    out_ref[s, 2, d, :] = value_grad[rows]

    half = max(ranks // 2, 1)

    @pl.loop(0, ranks)
    def _(rank):
        @pl.when((counts[rank] > 0) & (counts[rank] <= half))
        def _():
            variant(rank, half, half)

        @pl.when(counts[rank] > half)
        def _():
            variant(rank, ranks, half)


def attend(backward, ranks, run_count, run_rows, tables, *arrays):
    rows = run_count * run_rows
    shape = (ranks, 3, rows, HD) if backward else (ranks, rows, HD)
    vmem = pl.BlockSpec(memory_space=pltpu.VMEM)
    scratch = [pltpu.VMEM((ranks * run_rows, HD), F32)] * 2 if backward else []
    return pl.pallas_call(
        functools.partial(_attend_kernel, backward, ranks, run_count, run_rows),
        out_shape=jax.ShapeDtypeStruct(shape, BF),
        grid_spec=pltpu.PrefetchScalarGridSpec(
            num_scalar_prefetch=3,
            grid=(),
            in_specs=[vmem] * len(arrays),
            out_specs=vmem,
            scratch_shapes=scratch,
        ),
        compiler_params=pltpu.CompilerParams(vmem_limit_bytes=40 * 1024 * 1024),
        cost_estimate=pl.CostEstimate(
            flops=(6 if backward else 2) * 10**8, bytes_accessed=3 * 10**6, transcendentals=10**6
        ),
        name="attend_back" if backward else "attend",
    )(*tables, *arrays)


def run_tables(run_target, run_gather, ranks):
    runs = run_target.shape[0]
    rank_ids = jnp.arange(ranks, dtype=jnp.int32)
    named = run_target[None, :] == rank_ids[:, None]
    counts = jnp.sum(named.astype(jnp.int32), axis=1)
    run_ids = jnp.arange(runs, dtype=jnp.int32)
    earlier = named[:, None, :] & (run_ids[None, None, :] < run_ids[None, :, None])
    place = jnp.sum(earlier.astype(jnp.int32), axis=2)
    hit = named[:, None, :] & (place[:, None, :] == rank_ids[None, :, None])
    order = jnp.sum(jnp.where(hit, run_ids, 0), axis=2)
    gathers = jnp.sum(jnp.where(hit, run_gather + 1, 0), axis=2) - 1
    return counts, order.reshape(-1), gathers.reshape(-1)


def swap_gather(values, axis_name):
    if lax.axis_size(axis_name) != 2:
        return lax.all_gather(values, axis_name, axis=1, tiled=True)
    other = lax.ppermute(values, axis_name, [(0, 1), (1, 0)])
    first = lax.axis_index(axis_name) == 0
    return jnp.where(
        first,
        jnp.concatenate([values, other], axis=1),
        jnp.concatenate([other, values], axis=1),
    )


def on_device(projected, destinations, gather_ids, out_weight, grad_output):
    ranks = lax.axis_size("seq")
    row_count = projected.shape[0]
    run_rows = 2 * row_count // ranks
    run_count = row_count // run_rows
    width = projected.shape[2]
    exchange = functools.partial(
        lax.all_to_all, axis_name="seq", split_axis=0, concat_axis=0, tiled=True
    )
    run_info = jnp.concatenate(
        [
            destinations.reshape(run_count, run_rows)[:, 0],
            gather_ids.reshape(run_count, run_rows)[:, 0],
        ]
    )
    tail = jnp.broadcast_to(jnp.pad(run_info, (0, HD - 2 * run_count))[None, :], (16, HD))
    x = exchange(split_heads(projected.transpose(1, 0, 2), tail.astype(BF), ranks))
    info = x[:, 3 * row_count, : 2 * run_count].astype(jnp.int32)
    run_target = info[:, :run_count].reshape(-1)
    run_gather = info[:, run_count:].reshape(-1)
    tables = run_tables(run_target, run_gather, ranks)

    columns = swap_gather(grad_output, "tp")
    grad_rows = _dot(columns, out_weight, 1, 1).astype(BF)
    blocks = head_blocks(grad_rows, ranks)
    x, blocks, columns = lax.optimization_barrier((x, blocks, columns))
    g = exchange(blocks)

    attended = attend(False, ranks, run_count, run_rows, tables, x)
    attended_rows = exchange(attended)
    back = attend(True, ranks, run_count, run_rows, tables, x, attended, g)
    attended_rows, back = lax.optimization_barrier((attended_rows, back))
    grads = exchange(back)
    attended_rows = attended_rows.transpose(1, 0, 2).reshape(row_count, width)

    partial_terms = _dot(attended_rows, out_weight, 1, 0)
    product = _dot(attended_rows, columns, 0, 0)
    row_total = row_count * lax.axis_size("dp") * ranks
    half = out_weight.shape[1] // 2
    first = lax.axis_index("tp") == 0
    mine = jnp.where(first, partial_terms[:, :half], partial_terms[:, half:])
    sent = jnp.where(first, partial_terms[:, half:], partial_terms[:, :half]).astype(BF)
    other, total = reduce_sums(sent, product, ranks, 1.0 / math.sqrt(row_total))
    output = (mine + other.astype(F32)).astype(BF)
    grad_projected = join_heads(grads, row_count).transpose(1, 0, 2)
    return output, grad_projected, total.astype(F32)


def head_blocks(values, ranks):
    return jnp.stack([values[:, h * HD : (h + 1) * HD] for h in range(ranks)])


def _split_kernel(ranks, x_ref, tail_ref, out_ref):
    rows = x_ref.shape[1]
    for head in range(ranks):
        for part in range(3):
            block = x_ref[part, :, head * HD : (head + 1) * HD]
            out_ref[head, part * rows : (part + 1) * rows, :] = block
        out_ref[head, 3 * rows :, :] = tail_ref[...]


def split_heads(x, tail, ranks):
    vmem = pl.BlockSpec(memory_space=pltpu.VMEM)
    return pl.pallas_call(
        functools.partial(_split_kernel, ranks),
        out_shape=jax.ShapeDtypeStruct((ranks, 3 * x.shape[1] + tail.shape[0], HD), BF),
        in_specs=[vmem] * 2,
        out_specs=vmem,
        compiler_params=pltpu.CompilerParams(vmem_limit_bytes=24 * 1024 * 1024),
        cost_estimate=pl.CostEstimate(flops=0, bytes_accessed=4 * x.size, transcendentals=0),
        name="split_heads",
    )(x, tail)


def _join_kernel(x_ref, out_ref):
    for head in range(x_ref.shape[0]):
        for part in range(3):
            out_ref[part, :, head * HD : (head + 1) * HD] = x_ref[head, part]


def join_heads(x, rows):
    vmem = pl.BlockSpec(memory_space=pltpu.VMEM)
    return pl.pallas_call(
        _join_kernel,
        out_shape=jax.ShapeDtypeStruct((3, rows, x.shape[0] * HD), BF),
        in_specs=[vmem],
        out_specs=vmem,
        compiler_params=pltpu.CompilerParams(vmem_limit_bytes=24 * 1024 * 1024),
        cost_estimate=pl.CostEstimate(flops=0, bytes_accessed=4 * x.size, transcendentals=0),
        name="join_heads",
    )(x)


def _reduce_kernel(
    ranks, factor, sent_ref, product_ref, other_ref, out_ref, pair_out, pair_in, first_out, ring_in,
    tp_send, tp_recv, pair_send, pair_recv, sum_send, sum_recv, all_send, all_recv, last_send, last_recv
):
    core, seq, tp = lax.axis_index("dp"), lax.axis_index("seq"), lax.axis_index("tp")
    half, columns = product_ref.shape[0] // 2, product_ref.shape[1]
    chunk, wide = half // ranks, columns // 2
    mesh = pl.DeviceIdType.MESH

    def flip(index):
        z, x = index // 2, index % 2
        return z + x * (ranks - 1 - 2 * z)

    def unflip(place):
        x = place // (ranks // 2)
        return 2 * (place + x * (ranks - 1 - 2 * place)) + x

    me = flip(seq)
    ring = ({"seq": unflip((me + 1) % ranks)}, {"seq": unflip((me + ranks - 1) % ranks)})
    partner, across = {"dp": 1 - core}, {"tp": 1 - tp}

    barrier = pltpu.get_barrier_semaphore()
    for device in (*ring, partner, across):
        pl.semaphore_signal(barrier, inc=1, device_id=device, device_id_type=mesh)
    pl.semaphore_wait(barrier, 4)

    def send(source, target, send_sem, recv_sem, device):
        copy = pltpu.make_async_remote_copy(
            src_ref=source, dst_ref=target, send_sem=send_sem, recv_sem=recv_sem,
            device_id=device, device_id_type=mesh,
        )
        copy.start()
        return copy

    def place(offset):
        return (me + offset + ranks) % ranks

    def chunk_rows(start, index):
        return pl.ds(pl.multiple_of(start + index * chunk, chunk), chunk)

    offsets = sorted(range(1, ranks), key=lambda o: (min(o, ranks - o), o)) + [0]
    pair = {}
    for slot, offset in enumerate(offsets):
        rows = chunk_rows((1 - core) * half, place(offset))
        pair_out[slot] = product_ref[rows, :].astype(BF)
        pair[offset] = (
            slot,
            send(pair_out.at[slot], pair_in.at[slot], pair_send.at[slot], pair_recv.at[slot], partner),
        )
    crossing = send(sent_ref, other_ref, tp_send, tp_recv, across)
    here = set()

    def own(offset, cols):
        offset = offset % ranks
        slot, copy = pair[offset]
        if offset not in here:
            here.add(offset)
            copy.wait_recv()
        rows = chunk_rows(core * half, place(offset))
        return product_ref[rows, cols] + pair_in[slot, :, cols].astype(F32)

    cols = (slice(0, wide), slice(wide, columns))
    copies = []
    moving = [None, None]
    for way in range(2):
        sign = -1 if way == 0 else 1
        first_out[way] = own(sign, cols[way]).astype(BF)
        moving[way] = send(
            first_out.at[way], ring_in.at[way, 0], sum_send.at[way, 0], sum_recv.at[way, 0], ring[way]
        )
        copies.append(moving[way])
    for step in range(1, ranks):
        for way in range(2):
            sign = -1 if way == 0 else 1
            mine = own(sign * (step + 1), cols[way])
            moving[way].wait_recv()
            value = mine + ring_in[way, step - 1].astype(F32)
            if step < ranks - 1:
                ring_in[way, step - 1] = value.astype(BF)
                moving[way] = send(
                    ring_in.at[way, step - 1], ring_in.at[way, step],
                    sum_send.at[way, step], sum_recv.at[way, step], ring[way],
                )
                copies.append(moving[way])
            else:
                out_ref[chunk_rows(core * half, me), cols[way]] = (value * factor).astype(BF)

    arrived = [None, None]
    finals = []
    for step in range(ranks):
        for way in range(2):
            sign = -1 if way == 0 else 1
            if step > 0:
                arrived[way].wait_recv()
            view = out_ref.at[chunk_rows(core * half, place(sign * step)), cols[way]]
            if step < ranks - 1:
                arrived[way] = send(view, view, all_send.at[way, step], all_recv.at[way, step], ring[way])
                copies.append(arrived[way])
            final = send(view, view, last_send.at[way, step], last_recv.at[way, step], partner)
            finals.append(final)
    for copy in copies:
        copy.wait_send()
    for _, copy in pair.values():
        copy.wait_send()
    for copy in finals:
        copy.wait()
    crossing.wait()


def reduce_sums(sent, product, ranks, factor):
    half, columns = product.shape[0] // 2, product.shape[1]
    chunk = half // ranks
    dma = pltpu.SemaphoreType.DMA
    vmem = pl.BlockSpec(memory_space=pltpu.VMEM)
    return pl.pallas_call(
        functools.partial(_reduce_kernel, ranks, factor),
        out_shape=(
            jax.ShapeDtypeStruct(sent.shape, BF),
            jax.ShapeDtypeStruct(product.shape, BF),
        ),
        in_specs=[vmem] * 2,
        out_specs=(vmem, vmem),
        scratch_shapes=[
            pltpu.VMEM((ranks, chunk, columns), BF),
            pltpu.VMEM((ranks, chunk, columns), BF),
            pltpu.VMEM((2, chunk, columns // 2), BF),
            pltpu.VMEM((2, ranks - 1, chunk, columns // 2), BF),
            dma, dma,
            *[dma((ranks,))] * 2,
            *[dma((2, ranks))] * 6,
        ],
        compiler_params=pltpu.CompilerParams(
            collective_id=0, has_side_effects=True, vmem_limit_bytes=40 * 1024 * 1024
        ),
        cost_estimate=pl.CostEstimate(flops=6 * 10**10, bytes_accessed=2 * 10**7, transcendentals=0),
        name="reduce_sums",
    )(sent, product)


masked_score = -1e30


def packed_on_device(projected, destinations, gather_ids, out_weight, grad_output):
    rank_count = lax.axis_size("seq")
    row_count = projected.shape[0]
    run_rows = 2 * row_count // rank_count
    width_local = projected.shape[2]
    head_count = width_local // HD
    run_count = row_count // run_rows
    slot_count = rank_count * run_rows
    scaling = 1.0 / math.sqrt(HD)
    run_target = destinations.reshape(run_count, run_rows)[:, 0]
    run_gather = gather_ids.reshape(run_count, run_rows)[:, 0]
    picked_mask = run_target[None, :] == jnp.arange(rank_count, dtype=jnp.int32)[:, None]
    selector = picked_mask.astype(jnp.bfloat16)

    def pack_rows(values):
        features = values.shape[1]
        blocks = values.reshape(run_count, run_rows * features)
        packed = jnp.dot(selector, blocks, preferred_element_type=jnp.float32)
        return packed.astype(jnp.bfloat16).reshape(rank_count, run_rows, features)

    def unpack_rows(buffer):
        features = buffer.shape[2]
        flat = buffer.reshape(rank_count, run_rows * features)
        rows_back = lax.dot_general(
            selector, flat, (((0,), (0,)), ((), ())), preferred_element_type=jnp.float32
        )
        return rows_back.astype(jnp.bfloat16).reshape(row_count, features)

    slot_gather = jnp.where(
        jnp.any(picked_mask, axis=1),
        jnp.sum(jnp.where(picked_mask, run_gather[None, :], 0), axis=1),
        -1,
    )
    gather_send = jnp.broadcast_to(slot_gather[:, None], (rank_count, run_rows))
    packed_send = pack_rows(projected.reshape(row_count, 3 * width_local))
    received, received_ids = (
        lax.all_to_all(packed_send, "seq", split_axis=0, concat_axis=0, tiled=True),
        lax.all_to_all(gather_send, "seq", split_axis=0, concat_axis=0, tiled=True),
    )
    received = received.reshape(slot_count, 3, width_local)
    key_ids = received_ids.reshape(slot_count)
    matching = key_ids[:, None] == key_ids[None, :]

    def head_inputs(head_index):
        lower = head_index * HD
        return (
            received[:, 0, lower : lower + HD],
            received[:, 1, lower : lower + HD],
            received[:, 2, lower : lower + HD],
        )

    def probabilities(query_head, key_head):
        scores = (
            lax.dot_general(
                query_head, key_head, (((1,), (1,)), ((), ())), preferred_element_type=jnp.float32
            )
            * scaling
        )
        scores = jnp.where(matching, scores, masked_score)
        peak = jnp.max(scores, axis=1, keepdims=True)
        raised = jnp.exp(scores - peak)
        return raised / jnp.sum(raised, axis=1, keepdims=True)

    results = []
    for head_index in range(head_count):
        query_head, key_head, value_head = head_inputs(head_index)
        weights = probabilities(query_head, key_head).astype(jnp.bfloat16)
        results.append(
            jnp.dot(weights, value_head, preferred_element_type=jnp.float32).astype(jnp.bfloat16)
        )
    attended = jnp.concatenate(results, axis=1)
    returned = lax.all_to_all(
        attended.reshape(rank_count, run_rows, width_local),
        "seq",
        split_axis=0,
        concat_axis=0,
        tiled=True,
    )
    attended_rows = unpack_rows(returned)
    partial_terms = jnp.dot(attended_rows, out_weight, preferred_element_type=jnp.float32)
    output = lax.psum_scatter(partial_terms, "tp", scatter_dimension=1, tiled=True).astype(
        jnp.bfloat16
    )
    shard_cols = lax.all_gather(grad_output, "tp", axis=1, tiled=True)
    grad_rows = lax.dot_general(
        shard_cols, out_weight, (((1,), (1,)), ((), ())), preferred_element_type=jnp.float32
    )
    product = lax.dot_general(
        attended_rows, shard_cols, (((0,), (0,)), ((), ())), preferred_element_type=jnp.float32
    )
    grad_block = product
    grad_rows, grad_block = (grad_rows, grad_block)
    row_total = row_count * lax.axis_size("dp") * rank_count
    grad_weight = lax.psum(grad_block, ("dp", "seq")) * (1.0 / math.sqrt(row_total))
    grad_attended = grad_rows.astype(jnp.bfloat16)
    grad_slots = lax.all_to_all(
        pack_rows(grad_attended), "seq", split_axis=0, concat_axis=0, tiled=True
    )
    grad_slots = grad_slots.reshape(slot_count, width_local)
    query_grads = []
    key_grads = []
    value_grads = []
    for head_index in range(head_count):
        query_head, key_head, value_head = head_inputs(head_index)
        lower = head_index * HD
        grad_head = grad_slots[:, lower : lower + HD]
        result_head = attended[:, lower : lower + HD]
        weights = probabilities(query_head, key_head)
        weights_low = weights.astype(jnp.bfloat16)
        grad_weights = lax.dot_general(
            grad_head, value_head, (((1,), (1,)), ((), ())), preferred_element_type=jnp.float32
        )
        delta = jnp.sum(
            grad_head.astype(jnp.float32) * result_head.astype(jnp.float32), axis=1, keepdims=True
        )
        grad_scores = (weights * (grad_weights - delta)).astype(jnp.bfloat16)
        query_grads.append(
            (jnp.dot(grad_scores, key_head, preferred_element_type=jnp.float32) * scaling).astype(
                jnp.bfloat16
            )
        )
        key_grads.append(
            (
                lax.dot_general(
                    grad_scores,
                    query_head,
                    (((0,), (0,)), ((), ())),
                    preferred_element_type=jnp.float32,
                )
                * scaling
            ).astype(jnp.bfloat16)
        )
        value_grads.append(
            lax.dot_general(
                weights_low, grad_head, (((0,), (0,)), ((), ())), preferred_element_type=jnp.float32
            ).astype(jnp.bfloat16)
        )
    stacked = jnp.stack(
        [
            jnp.concatenate(query_grads, axis=1),
            jnp.concatenate(key_grads, axis=1),
            jnp.concatenate(value_grads, axis=1),
        ],
        axis=1,
    )
    grads_back = lax.all_to_all(
        stacked.reshape(rank_count, run_rows, 3 * width_local),
        "seq",
        split_axis=0,
        concat_axis=0,
        tiled=True,
    )
    grad_projected = unpack_rows(grads_back).reshape(row_count, 3, width_local)
    return (output, grad_projected, grad_weight)


def solution(mesh):
    placed = (
        P(("dp", "seq"), None, "tp"),
        P(("dp", "seq")),
        P(("dp", "seq")),
        P("tp", None),
        P(("dp", "seq"), "tp"),
    )
    sizes = mesh.shape
    whole_heads = 2048 // HD // sizes["tp"] == sizes["seq"] and sizes["tp"] == 2 == sizes["dp"]
    return jax.shard_map(
        on_device if whole_heads else packed_on_device,
        mesh=mesh,
        in_specs=placed,
        out_specs=(P(("dp", "seq"), "tp"), P(("dp", "seq"), None, "tp"), P("tp", None)),
        check_vma=False,
    )
```
